32 devices in a mesh: replica: 2 (over x), node: 2 (over core), local: 8 (over z, y).
Axes of the slice: x: 2, y: 2, z: 4, core: 2. Of those that a mesh axis runs over, the one named last changes fastest.
Arguments:
- tokens: bfloat16 [2048, 3584], P(('replica', 'node', 'local')), parts along dimension 0, may hold values from -6 to 6
- expert_ids: int32 [2048, 4], P(('replica', 'node', 'local')), parts along dimension 0, may hold values from 0 to 7, all different within a row; in each aligned block of 64 rows (0 to 63, 64 to 127, ...) at most 48 rows name the same one
- combine_weights: bfloat16 [2048, 4], P(('replica', 'node', 'local')), parts along dimension 0, may hold values from 0.099609375 to 1
- w_gate: bfloat16 [16, 3584, 512], P(('node', 'local')), may hold values from -0.09375 to 0.09375
- w_up: bfloat16 [16, 3584, 512], P(('node', 'local')), may hold values from -0.09375 to 0.09375
- w_down: bfloat16 [16, 512, 3584], P(('node', 'local')), may hold values from -0.1875 to 0.1875
- queries: bfloat16 [2048, 64, 576], P(('replica', 'node', 'local')), parts along dimension 0, may hold values from -400 to 400
- latent_cache: bfloat16 [2048, 64, 576], P(('replica', 'node', 'local')), parts along dimension 0, may hold values from -6 to 6
- cache_lengths: int32 [2048], P(('replica', 'node', 'local')), parts along dimension 0, may hold values from 2 to 64, as said below
Outputs:
- moe_out: bfloat16 [2048, 3584], P(('replica', 'node', 'local')), parts along dimension 0
- attn_latent: bfloat16 [2048, 64, 512], P(('replica', 'node', 'local')), parts along dimension 0
The draws below stay inside these ranges and needn't reach their ends.
There are 2 independent parts, one for each index of `replica`. The reference program is written for one: setup_inputs(seed, part) draws one part's arguments, and reference() takes and returns one part's arrays. A program takes and returns all parts, laid end to end along the dimension named above; an argument that names none is the same for every part. Nothing has to cross between parts.
Inputs may be any that keep to these rules, and one draw needn't show every extreme that they name: `expert_ids`: each row names 4 different experts; among the rows of one device no expert is named more than 48 times, and some device names some expert exactly 48 times. `cache_lengths`: some sequence has exactly 64 live positions.
All inputs are finite; a program needn't handle non-finite values.
Results may differ from the reference program's by a relative error of at most 0.0085.
Values may be sent and summed in bfloat16 or wider, within the bound.
No kernel may reach another device: no remote copies, remote signals or barrier semaphores. Data moves between devices by JAX's collectives and lax.ppermute only.
A program may use at most 128 MiB of HBM per device.

```python
import math
import jax
import jax.numpy as jnp
import numpy as np
from jax import lax

D = 3584
FF = 1024
HEADS = 64
LAT = 512
ROPE = 64
TOPK = 4
TOK_DEV = 64
CACHE = 64
EXPERTS = 8
CAP = 48
TOKENS = 1024
N_NODE = 2
N_LOCAL = 8


def latent_draw(key):
    return jnp.clip(jax.random.normal(jax.random.fold_in(key, 17), (TOKENS, CACHE, LAT + ROPE), jnp.float32), -6.0, 6.0)


def draw_latent_cache(key, part):
    latent_base = latent_draw(key)
    return latent_base.astype(jnp.bfloat16)


def draw_queries(key, part):
    key = jax.random.fold_in(key, 5)
    fresh_draw = jnp.clip(jax.random.normal(key, (TOKENS, HEADS, LAT + ROPE), jnp.float32), -6.0, 6.0)
    return fresh_draw.astype(jnp.bfloat16)


def draw_cache_lengths(key, part):
    key = jax.random.fold_in(key, 7)
    lengths = jax.random.randint(key, (TOKENS,), 2, CACHE + 1)
    longest = jax.random.randint(jax.random.fold_in(key, 1), (), 0, TOKENS)
    return lengths.at[longest].set(CACHE).astype(jnp.int32)


def levels(stream_key, extent, pieces, least, largest):
    gain = 1.0
    for axis_at, blocks in pieces:
        draws = jax.random.uniform(jax.random.fold_in(jax.random.fold_in(stream_key, 6), axis_at), (blocks,), jnp.float32, least / len(pieces), largest / len(pieces))
        gain = gain * jnp.repeat(jnp.exp(draws), extent[axis_at] // blocks).reshape((-1,) + (1,) * (len(extent) - 1 - axis_at))
    return gain


def shared_out(key, own, number, rows, count, top, limit, lean):
    sequence = jax.random.permutation(key, count)
    crowded, usual = portions_of(count, rows * top, limit, lean, True), portions_of(count, rows * top, limit, lean, False)
    places = jnp.arange(count)

    def named(sizes, offset_by):
        used = int((sizes > 0).sum())
        fixed = max(1, used // 4)
        passed = fixed + (places - fixed + offset_by * (used - fixed)) % max(1, count - fixed)
        return jnp.zeros((count,), jnp.int32).at[sequence[jnp.where(places < fixed, places, passed)]].set(jnp.asarray(sizes, jnp.int32))

    sizes = jnp.where(number % 4 == 0, named(crowded, number // 4), named(usual, number - number // 4 - 1))
    mixed = jax.random.permutation(jax.random.fold_in(own, 3), count)
    giver, sink = mixed[0:count // 2 * 2:2], mixed[1:count // 2 * 2:2]
    room = jnp.minimum(sizes[giver] - 1, limit - sizes[sink]) // 2
    room = jnp.where((giver == sequence[0]) | (sink == sequence[0]) | (sizes[sink] == 0), 0, jnp.maximum(room, 0))
    passed = jax.random.randint(jax.random.fold_in(own, 4), (count // 2,), 0, 1 << 20) % (room + 1)
    sizes = sizes.at[giver].add(-passed).at[sink].add(passed)
    items = jnp.searchsorted(jnp.cumsum(sizes), jnp.arange(rows * top), side="right").astype(jnp.int32)
    grid = items.reshape(top, rows).T
    grid = grid[jax.random.permutation(jax.random.fold_in(own, 1), rows)]
    offset_by = jax.random.randint(jax.random.fold_in(own, 2), (rows, 1), 0, top)
    return jnp.take_along_axis(grid, (jnp.arange(top)[None, :] + offset_by) % top, axis=1)


def portions_of(amount, total, bound, lean, full):
    loads = [(1 << 20) // math.isqrt(rank ** lean) + 1 for rank in range(1, amount + 1)]
    largest = bound if full else min(bound, max(-(-total // amount), total * loads[0] // sum(loads)))
    least = 1 if total - largest >= amount - 1 else 0
    holding, rest = [largest] + [least] * (amount - 1), total - largest - least * (amount - 1)
    while rest > 0:
        movable = [i for i in range(1, amount) if holding[i] < largest] or [i for i in range(1, amount) if holding[i] < bound]
        pool, remaining = sum([loads[i] for i in movable]), rest
        for i in movable:
            more = min(bound - holding[i], max(1, remaining * loads[i] // pool), rest)
            holding[i] = holding[i] + more
            rest = rest - more
    return np.array(holding)


def bell_draw(key, dims, spread, most, split=(), kind=jnp.bfloat16):
    level = levels(key, dims, split, -0.22, 0.18) if split else 1.0
    entries = jax.random.normal(key, dims, jnp.float32) * spread * level
    return jnp.minimum(jnp.maximum(entries, -most), most).astype(kind)


def setup_inputs(seed: int = 0, part: int = 0) -> dict:
    streams_of = jax.random.split(jax.random.key(seed), 10)
    part_splits = jax.random.split(jax.random.fold_in(streams_of[9], part), 10)
    tokens = bell_draw(part_splits[0], (TOKENS, D), 1.0, 6.0, ((0, 16),))
    expert_ids_keys = jax.random.split(jax.random.fold_in(part_splits[1], 1), TOKENS // TOK_DEV)
    expert_ids_turns = jax.random.permutation(jax.random.fold_in(part_splits[1], 3), TOKENS // TOK_DEV)
    expert_ids = jax.vmap(lambda own, number: shared_out(jax.random.fold_in(part_splits[1], 2), own, number, TOK_DEV, EXPERTS, TOPK, CAP, 2))(expert_ids_keys, expert_ids_turns).reshape((TOKENS, TOPK))
    combine_weights = jnp.clip(jnp.exp(math.log(1.0) - 2.306499 * jax.random.uniform(part_splits[2], (TOKENS, TOPK), jnp.float32) ** levels(part_splits[2], (TOKENS, TOPK), ((0, 16),), -0.2, 0.2)), 0.099609375, 1.0).astype(jnp.bfloat16)
    w_gate = bell_draw(streams_of[3], (EXPERTS * 2, D, FF // 2), D ** -0.5, 0.09375, ((0, 16),))
    w_up = bell_draw(streams_of[4], (EXPERTS * 2, D, FF // 2), D ** -0.5, 0.09375, ((0, 16),))
    w_down = bell_draw(streams_of[5], (EXPERTS * 2, FF // 2, D), FF ** -0.5, 0.1875, ((0, 16),))
    queries = draw_queries(jax.random.fold_in(jax.random.fold_in(streams_of[9], part), 71), part)
    latent_cache = draw_latent_cache(jax.random.fold_in(jax.random.fold_in(streams_of[9], part), 71), part)
    cache_lengths = draw_cache_lengths(jax.random.fold_in(jax.random.fold_in(streams_of[9], part), 71), part)
    return {"tokens": tokens, "expert_ids": expert_ids, "combine_weights": combine_weights, "w_gate": w_gate, "w_up": w_up, "w_down": w_down, "queries": queries, "latent_cache": latent_cache, "cache_lengths": cache_lengths}


SOFTMAX_SCALE = 192.0 ** -0.5


def expert_half(slot_rows, slot_weights, gate_half, up_half, down_half):
    gate_out = jnp.dot(slot_rows, gate_half, preferred_element_type=jnp.float32)
    up_out = jnp.dot(slot_rows, up_half, preferred_element_type=jnp.float32)
    hidden = (jax.nn.silu(gate_out) * up_out).astype(jnp.bfloat16)
    down_out = jnp.dot(hidden, down_half, preferred_element_type=jnp.float32)
    return (slot_weights.astype(jnp.float32)[:, None] * down_out).astype(jnp.bfloat16)


def mixture(tokens, expert_ids, combine_weights, w_gate, w_up, w_down):
    expert_count = N_NODE * N_LOCAL // 2
    per_node = expert_count // N_NODE
    pick_total = N_NODE * N_LOCAL * CAP
    matches = expert_ids[:, :, None] == jnp.arange(expert_count, dtype=jnp.int32)[None, None, :]
    route_weight = jnp.sum(jnp.where(matches, combine_weights[:, :, None], jnp.zeros((), jnp.bfloat16)), axis=1)
    padded_rows = jnp.concatenate([tokens, jnp.zeros((1, D), jnp.bfloat16)], axis=0)
    padded_weight = jnp.concatenate([route_weight, jnp.zeros((1, expert_count), jnp.bfloat16)], axis=0)

    def one_expert(expert, node_sums):
        column = lax.dynamic_index_in_dim(route_weight, expert, 1, keepdims=False)
        chosen = jnp.nonzero(column != 0, size=pick_total, fill_value=TOKENS)[0].astype(jnp.int32)
        slot_rows = padded_rows[chosen]
        slot_weights = lax.dynamic_index_in_dim(padded_weight, expert, 1, keepdims=False)[chosen]
        node_of = expert // per_node
        for half_index in range(2):
            layer_index = 2 * expert + half_index
            partial_out = expert_half(slot_rows, slot_weights, w_gate[layer_index], w_up[layer_index], w_down[layer_index])
            widened = lax.optimization_barrier(partial_out).astype(jnp.float32)
            node_sums = node_sums.at[node_of, chosen].add(widened)
        return node_sums

    node_sums = lax.fori_loop(0, expert_count, one_expert, jnp.zeros((N_NODE, TOKENS + 1, D), jnp.float32))
    rounded = lax.optimization_barrier(node_sums[:, :TOKENS].astype(jnp.bfloat16)).astype(jnp.float32)
    return jnp.sum(rounded, axis=0).astype(jnp.bfloat16)


def attend(queries, latent_cache, cache_lengths):
    scores = SOFTMAX_SCALE * jnp.einsum("thc,tjc->thj", queries.astype(jnp.float32), latent_cache.astype(jnp.float32))
    valid_mask = (jnp.arange(latent_cache.shape[1])[None, :] < cache_lengths[:, None])[:, None, :]
    scores = jnp.where(valid_mask, scores, -1e30)
    row_peak = jnp.max(scores, axis=2, keepdims=True)
    exp_terms = jnp.where(valid_mask, jnp.exp(scores - row_peak), 0.0)
    attn_probs = (exp_terms / jnp.sum(exp_terms, axis=2, keepdims=True)).astype(jnp.bfloat16)
    latent_values = latent_cache[:, :, :LAT]
    return jnp.einsum("thj,tjc->thc", attn_probs.astype(jnp.float32), latent_values.astype(jnp.float32)).astype(jnp.bfloat16)


def reference(tokens, expert_ids, combine_weights, w_gate, w_up, w_down, queries, latent_cache, cache_lengths):
    moe_out = mixture(tokens, expert_ids, combine_weights, w_gate, w_up, w_down)
    attn_latent = attend(queries, latent_cache, cache_lengths)
    return (moe_out, attn_latent)
```

```python
import jax
import jax.numpy as jnp
from jax import lax
from jax.sharding import PartitionSpec as P

LAT = 512
SOFTMAX_SCALE = 192.0 ** (-0.5)
LANES = 128


def attend(queries, latent_cache, cache_lengths, latent_width):
    scores = SOFTMAX_SCALE * jnp.einsum(
        "thc,tjc->thj", queries, latent_cache, preferred_element_type=jnp.float32
    )
    valid_mask = (jnp.arange(latent_cache.shape[1])[None, :] < cache_lengths[:, None])[:, None, :]
    scores = jnp.where(valid_mask, scores, -1e30)
    row_peak = jnp.max(scores, axis=2, keepdims=True)
    exp_terms = jnp.where(valid_mask, jnp.exp(scores - row_peak), 0.0)
    attn_probs = (exp_terms / jnp.sum(exp_terms, axis=2, keepdims=True)).astype(jnp.bfloat16)
    return jnp.einsum(
        "thj,tjc->thc",
        attn_probs,
        latent_cache[:, :, :latent_width],
        preferred_element_type=jnp.float32,
    ).astype(jnp.bfloat16)


def ring_order(count):
    if count == 8:
        return [0, 2, 4, 6, 7, 5, 3, 1]
    return list(range(count))


def on_device(
    tokens, expert_ids, combine_weights, w_gate, w_up, w_down, queries, latent_cache, cache_lengths
):
    node_count = lax.axis_size("node")
    local_count = lax.axis_size("local")
    expert_count = node_count * local_count // 2
    rows, width = tokens.shape
    half = local_count // 2
    order = ring_order(local_count)
    forward = [(order[i], order[(i + 1) % local_count]) for i in range(local_count)]
    backward = [(b, a) for a, b in forward]
    swap = [(i, (i + 1) % node_count) for i in range(node_count)]
    device_index = lax.axis_index("node") * local_count + lax.axis_index("local")
    expert = device_index // 2

    matches = expert_ids[:, :, None] == jnp.arange(LANES, dtype=jnp.int32)[None, None, :]
    route = jnp.sum(
        jnp.where(matches, combine_weights[:, :, None], jnp.zeros((), jnp.bfloat16)), axis=1
    )
    mine = jnp.concatenate([tokens, route], axis=1)

    def cw(a):
        return lax.ppermute(a, "local", forward)

    def ccw(a):
        return lax.ppermute(a, "local", backward)

    def across(a):
        return lax.ppermute(a, "node", swap)

    groups = [mine]
    behind, ahead = mine, mine
    for k in range(1, half + 1):
        if k == half:
            behind, ahead = behind[: rows // 2], ahead[rows // 2 :]
        behind, ahead = cw(behind), ccw(ahead)
        groups.append(jnp.concatenate([behind, ahead], axis=0))

    def experts(block):
        x = block[:, :width]
        weight = jnp.sum(
            jnp.where(
                jnp.arange(LANES)[None, :] == expert, block[:, width:].astype(jnp.float32), 0.0
            ),
            axis=1,
            keepdims=True,
        )
        gate_out = jnp.dot(x, w_gate[0], preferred_element_type=jnp.float32)
        up_out = jnp.dot(x, w_up[0], preferred_element_type=jnp.float32)
        hidden = (jax.nn.silu(gate_out) * up_out).astype(jnp.bfloat16)
        down = jnp.dot(hidden, w_down[0], preferred_element_type=jnp.float32)
        return (weight * down).astype(jnp.bfloat16)

    sums = []
    for group in groups:
        count = group.shape[0]
        both = jnp.concatenate([group, across(group)], axis=0)
        out = experts(both)
        sums.append(out[:count].astype(jnp.float32) + across(out[count:]).astype(jnp.float32))

    far = sums[half].astype(jnp.bfloat16)
    to_ahead, to_behind = cw(far[: rows // 2]), ccw(far[rows // 2 :])
    for k in range(half - 1, 0, -1):
        own_behind, own_ahead = sums[k][:rows], sums[k][rows:]
        if k == half - 1:
            zero = jnp.zeros_like(to_ahead)
            to_ahead = jnp.concatenate([to_ahead, zero], axis=0)
            to_behind = jnp.concatenate([zero, to_behind], axis=0)
        to_ahead = cw((own_ahead + to_ahead.astype(jnp.float32)).astype(jnp.bfloat16))
        to_behind = ccw((own_behind + to_behind.astype(jnp.float32)).astype(jnp.bfloat16))
    moe_out = (
        sums[0] + to_ahead.astype(jnp.float32) + to_behind.astype(jnp.float32)
    ).astype(jnp.bfloat16)

    attn_latent = attend(queries, latent_cache, cache_lengths, LAT)
    return (moe_out, attn_latent)


def solution(mesh):
    in_specs = (
        P(("replica", "node", "local"), None),
        P(("replica", "node", "local"), None),
        P(("replica", "node", "local"), None),
        P(("node", "local"), None, None),
        P(("node", "local"), None, None),
        P(("node", "local"), None, None),
        P(("replica", "node", "local"), None, None),
        P(("replica", "node", "local"), None, None),
        P(("replica", "node", "local")),
    )
    out_specs = (P(("replica", "node", "local"), None), P(("replica", "node", "local"), None, None))
    return jax.shard_map(
        on_device, mesh=mesh, in_specs=in_specs, out_specs=out_specs, check_vma=False
    )
```

```python
import jax
import jax.numpy as jnp
from jax import lax
from jax.experimental import pallas as pl
from jax.experimental.pallas import tpu as pltpu
from jax.sharding import PartitionSpec as P

LAT = 512
SOFTMAX_SCALE = 192.0 ** (-0.5)
LANES = 128


def attend(queries, latent_cache, cache_lengths, latent_width):
    scores = SOFTMAX_SCALE * jnp.einsum(
        "thc,tjc->thj", queries, latent_cache, preferred_element_type=jnp.float32
    )
    valid_mask = (jnp.arange(latent_cache.shape[1])[None, :] < cache_lengths[:, None])[:, None, :]
    scores = jnp.where(valid_mask, scores, -1e30)
    row_peak = jnp.max(scores, axis=2, keepdims=True)
    exp_terms = jnp.where(valid_mask, jnp.exp(scores - row_peak), 0.0)
    attn_probs = (exp_terms / jnp.sum(exp_terms, axis=2, keepdims=True)).astype(jnp.bfloat16)
    return jnp.einsum(
        "thj,tjc->thc",
        attn_probs,
        latent_cache[:, :, :latent_width],
        preferred_element_type=jnp.float32,
    ).astype(jnp.bfloat16)


def expert_kernel(expert_ref, own_ref, other_ref, gate_ref, up_ref, down_ref, own_out, other_out):
    rows, width = own_out.shape
    x = jnp.concatenate([own_ref[:, :width], other_ref[:, :width]], axis=0)
    gate = jnp.dot(x, gate_ref[...], preferred_element_type=jnp.float32)
    up = jnp.dot(x, up_ref[...], preferred_element_type=jnp.float32)
    hidden = (gate / (1.0 + jnp.exp(-gate)) * up).astype(jnp.bfloat16)
    down = jnp.dot(hidden, down_ref[...], preferred_element_type=jnp.float32)
    lane = lax.broadcasted_iota(jnp.int32, (rows, LANES), 1)
    for at, source, out in ((0, own_ref, own_out), (rows, other_ref, other_out)):
        route = source[:, width:].astype(jnp.float32)
        weight = jnp.sum(jnp.where(lane == expert_ref[0], route, 0.0), axis=1, keepdims=True)
        out[...] = (weight * down[at : at + rows]).astype(jnp.bfloat16)


def run_experts(expert, own, other, gate, up, down):
    rows, wide = own.shape
    width, hidden = gate.shape

    def whole(shape):
        return pl.BlockSpec(shape, lambda i, e: (0, 0))

    return pl.pallas_call(
        expert_kernel,
        grid_spec=pltpu.PrefetchScalarGridSpec(
            num_scalar_prefetch=1,
            grid=(1,),
            in_specs=[
                whole((rows, wide)),
                whole((rows, wide)),
                whole((width, hidden)),
                whole((width, hidden)),
                whole((hidden, width)),
            ],
            out_specs=[whole((rows, width)), whole((rows, width))],
        ),
        out_shape=[jax.ShapeDtypeStruct((rows, width), jnp.bfloat16)] * 2,
        compiler_params=pltpu.CompilerParams(vmem_limit_bytes=16 << 20),
        cost_estimate=pl.CostEstimate(
            flops=12 * rows * width * hidden,
            bytes_accessed=6 * width * hidden,
            transcendentals=2 * rows * hidden,
        ),
        name="expert_half",
    )(expert, own, other, gate, up, down)


def ring_order(count):
    if count == 8:
        return [0, 2, 4, 6, 7, 5, 3, 1]
    return list(range(count))


def on_device(
    tokens, expert_ids, combine_weights, w_gate, w_up, w_down, queries, latent_cache, cache_lengths
):
    local_count = lax.axis_size("local")
    rows, width = tokens.shape
    part = rows // 2
    node = lax.axis_index("node")
    order = ring_order(local_count)
    hops = []
    for i in range(local_count):
        here, there = order[i], order[(i + 1) % local_count]
        hops.append((here, there))
        hops.append((local_count + there, local_count + here))
    expert = ((node * local_count + lax.axis_index("local")) // 2).astype(jnp.int32).reshape(1)

    def onward(a):
        return lax.ppermute(a, ("node", "local"), hops)

    def across(a):
        return lax.ppermute(a, "node", [(0, 1), (1, 0)])

    matches = expert_ids[:, :, None] == jnp.arange(LANES, dtype=jnp.int32)[None, None, :]
    route = jnp.sum(
        jnp.where(matches, combine_weights[:, :, None], jnp.zeros((), jnp.bfloat16)), axis=1
    )
    mine = jnp.concatenate([tokens, route], axis=1)
    first = node == 0
    kept = jnp.where(first, mine[:part], mine[part:])
    given = jnp.where(first, mine[part:], mine[:part])
    gate, up, down = [
        pltpu.with_memory_space_constraint(w[0], pltpu.VMEM) for w in (w_gate, w_up, w_down)
    ]

    block = jnp.concatenate([kept, across(given)], axis=0)
    own_sums, other_sums = [], []
    for k in range(local_count):
        if k:
            block = onward(block)
        own, other = run_experts(expert, block, across(block), gate, up, down)
        own_sums.append(own)
        other_sums.append(across(other))

    def chip_sum(k):
        return own_sums[k].astype(jnp.float32) + other_sums[k].astype(jnp.float32)

    running = chip_sum(1).astype(jnp.bfloat16)
    for k in range(2, local_count):
        running = (chip_sum(k) + onward(running).astype(jnp.float32)).astype(jnp.bfloat16)
    total = (chip_sum(0) + onward(running).astype(jnp.float32)).astype(jnp.bfloat16)
    mine_out, back = total[:part], across(total[part:])
    moe_out = jnp.where(
        first,
        jnp.concatenate([mine_out, back], axis=0),
        jnp.concatenate([back, mine_out], axis=0),
    )

    attn_latent = attend(queries, latent_cache, cache_lengths, LAT)
    return (moe_out, attn_latent)


def solution(mesh):
    in_specs = (
        P(("replica", "node", "local"), None),
        P(("replica", "node", "local"), None),
        P(("replica", "node", "local"), None),
        P(("node", "local"), None, None),
        P(("node", "local"), None, None),
        P(("node", "local"), None, None),
        P(("replica", "node", "local"), None, None),
        P(("replica", "node", "local"), None, None),
        P(("replica", "node", "local")),
    )
    out_specs = (P(("replica", "node", "local"), None), P(("replica", "node", "local"), None, None))
    return jax.shard_map(
        on_device, mesh=mesh, in_specs=in_specs, out_specs=out_specs, check_vma=False
    )
```

```python
import jax
import jax.numpy as jnp
from jax import lax
from jax.experimental import pallas as pl
from jax.experimental.pallas import tpu as pltpu
from jax.sharding import PartitionSpec as P

LAT = 512
SOFTMAX_SCALE = 192.0 ** (-0.5)
LANES = 128


def attention_probs(queries, latent_cache, cache_lengths):
    scores = SOFTMAX_SCALE * jnp.einsum(
        "thc,tjc->thj", queries, latent_cache, preferred_element_type=jnp.float32
    )
    valid_mask = (jnp.arange(latent_cache.shape[1])[None, :] < cache_lengths[:, None])[:, None, :]
    scores = jnp.where(valid_mask, scores, -1e30)
    row_peak = jnp.max(scores, axis=2, keepdims=True)
    exp_terms = jnp.where(valid_mask, jnp.exp(scores - row_peak), 0.0)
    return (exp_terms / jnp.sum(exp_terms, axis=2, keepdims=True)).astype(jnp.bfloat16)


def expert_kernel(expert_ref, own_ref, other_ref, gate_ref, up_ref, down_ref, *rest):
    own_out, other_out = rest[-2:]
    rows, width = own_out.shape
    x = jnp.concatenate([own_ref[:, :width], other_ref[:, :width]], axis=0)
    gate = jnp.dot(x, gate_ref[...], preferred_element_type=jnp.float32)
    up = jnp.dot(x, up_ref[...], preferred_element_type=jnp.float32)
    hidden = (gate / (1.0 + jnp.exp(-gate)) * up).astype(jnp.bfloat16)
    down = jnp.dot(hidden, down_ref[...], preferred_element_type=jnp.float32)
    lane = lax.broadcasted_iota(jnp.int32, (rows, LANES), 1)
    for at, source, out in ((0, own_ref, own_out), (rows, other_ref, other_out)):
        route = source[:, width:].astype(jnp.float32)
        weight = jnp.sum(jnp.where(lane == expert_ref[0], route, 0.0), axis=1, keepdims=True)
        out[...] = (weight * down[at : at + rows]).astype(jnp.bfloat16)


def run_experts(expert, own, other, gate, up, down, after=()):
    rows, wide = own.shape
    width, hidden = gate.shape

    def whole(shape):
        return pl.BlockSpec(shape, lambda i, e: (0, 0))

    return pl.pallas_call(
        expert_kernel,
        grid_spec=pltpu.PrefetchScalarGridSpec(
            num_scalar_prefetch=1,
            grid=(1,),
            in_specs=[
                whole((rows, wide)),
                whole((rows, wide)),
                whole((width, hidden)),
                whole((width, hidden)),
                whole((hidden, width)),
            ]
            + [pl.BlockSpec(memory_space=pl.ANY)] * len(after),
            out_specs=[whole((rows, width)), whole((rows, width))],
        ),
        out_shape=[jax.ShapeDtypeStruct((rows, width), jnp.bfloat16)] * 2,
        compiler_params=pltpu.CompilerParams(vmem_limit_bytes=16 << 20),
        cost_estimate=pl.CostEstimate(
            flops=12 * rows * width * hidden,
            bytes_accessed=6 * width * hidden,
            transcendentals=2 * rows * hidden,
        ),
        name="expert_half",
    )(expert, own, other, gate, up, down, *after)


def ring_order(count):
    if count == 8:
        return [0, 2, 4, 6, 7, 5, 3, 1]
    return list(range(count))


def on_device(
    tokens, expert_ids, combine_weights, w_gate, w_up, w_down, queries, latent_cache, cache_lengths
):
    local_count = lax.axis_size("local")
    rows, width = tokens.shape
    part = rows // 2
    node = lax.axis_index("node")
    order = ring_order(local_count)
    hops, hops_in, hops_out = [], [], []
    for i in range(local_count):
        here, there = order[i], order[(i + 1) % local_count]
        hops += [(here, there), (local_count + there, local_count + here)]
        hops_in += [(local_count + here, there), (there, local_count + here)]
        hops_out += [(here, local_count + there), (local_count + there, here)]
    expert = ((node * local_count + lax.axis_index("local")) // 2).astype(jnp.int32).reshape(1)

    def onward(a, pairs=hops):
        return lax.ppermute(a, ("node", "local"), pairs)

    def across(a):
        return lax.ppermute(a, "node", [(0, 1), (1, 0)])

    matches = expert_ids[:, :, None] == jnp.arange(LANES, dtype=jnp.int32)[None, None, :]
    route = jnp.sum(
        jnp.where(matches, combine_weights[:, :, None], jnp.zeros((), jnp.bfloat16)), axis=1
    )
    mine = jnp.concatenate([tokens, route], axis=1)
    first = node == 0
    kept = jnp.where(first, mine[:part], mine[part:])
    given = jnp.where(first, mine[part:], mine[:part])
    gate, up, down = w_gate[0], w_up[0], w_down[0]

    block = jnp.concatenate([onward(kept), onward(given, hops_in)], axis=0)
    probs = attention_probs(queries, latent_cache, cache_lengths)
    own, other = run_experts(expert, mine, across(mine), gate, up, down)
    own_sums, other_sums = [own], [across(other)]
    after = (own, probs)
    for k in range(1, local_count):
        if k > 1:
            block = onward(block)
        own, other = run_experts(expert, block, across(block), gate, up, down, after)
        own_sums.append(own)
        other_sums.append(across(other))
        after = ()

    def chip_sum(k):
        return own_sums[k].astype(jnp.float32) + other_sums[k].astype(jnp.float32)

    running = chip_sum(1).astype(jnp.bfloat16)
    for k in range(2, local_count):
        running = (chip_sum(k) + onward(running).astype(jnp.float32)).astype(jnp.bfloat16)
    same, cross = onward(running[:part]), onward(running[part:], hops_out)
    arrived = jnp.where(
        first, jnp.concatenate([same, cross], axis=0), jnp.concatenate([cross, same], axis=0)
    )
    moe_out = (chip_sum(0) + arrived.astype(jnp.float32)).astype(jnp.bfloat16)

    attn_latent = jnp.einsum(
        "thj,tjc->thc", probs, latent_cache[:, :, :LAT], preferred_element_type=jnp.float32
    ).astype(jnp.bfloat16)
    return (moe_out, attn_latent)


def solution(mesh):
    in_specs = (
        P(("replica", "node", "local"), None),
        P(("replica", "node", "local"), None),
        P(("replica", "node", "local"), None),
        P(("node", "local"), None, None),
        P(("node", "local"), None, None),
        P(("node", "local"), None, None),
        P(("replica", "node", "local"), None, None),
        P(("replica", "node", "local"), None, None),
        P(("replica", "node", "local")),
    )
    out_specs = (P(("replica", "node", "local"), None), P(("replica", "node", "local"), None, None))
    return jax.shard_map(
        on_device, mesh=mesh, in_specs=in_specs, out_specs=out_specs, check_vma=False
    )
```

```python
import functools

import jax
import jax.numpy as jnp
from jax import lax
from jax.experimental import pallas as pl
from jax.experimental.pallas import tpu as pltpu
from jax.sharding import PartitionSpec as P

LAT = 512
SOFTMAX_SCALE = 192.0 ** (-0.5)
LANES = 128
PIECES = 4


def attend_kernel(len_ref, q_ref, c_ref, *rest, base, pair):
    done_ref = rest[-1]
    done_ref[...] = jnp.zeros_like(done_ref)
    out_ref = rest[-2]
    step, heads, wide = q_ref.shape
    slots = c_ref.shape[1]
    lat = out_ref.shape[2]
    row = lax.broadcasted_iota(jnp.int32, (pair * heads, pair * slots), 0) // heads
    col = lax.broadcasted_iota(jnp.int32, (pair * heads, pair * slots), 1)
    place = jnp.where(col // slots == row, col % slots, slots)
    which = lax.broadcasted_iota(jnp.int32, (pair * heads, 1), 0) // heads
    groups = range(0, step, pair)
    caches = [c_ref[at : at + pair].reshape(pair * slots, wide) for at in groups]
    scores = [
        lax.dot_general(
            q_ref[at : at + pair].reshape(pair * heads, wide),
            cache,
            (((1,), (1,)), ((), ())),
            preferred_element_type=jnp.float32,
        )
        for at, cache in zip(groups, caches, strict=True)
    ]
    probs = []
    for at, score in zip(groups, scores, strict=True):
        live = jnp.full((pair * heads, 1), len_ref[base + at], jnp.int32)
        for j in range(1, pair):
            live = jnp.where(which == j, len_ref[base + at + j], live)
        score = jnp.where(place < live, score * SOFTMAX_SCALE, -1e30)
        terms = jnp.exp(score - jnp.max(score, axis=1, keepdims=True))
        probs.append((terms * (1.0 / jnp.sum(terms, axis=1, keepdims=True))).astype(jnp.bfloat16))
    for at, prob, cache in zip(groups, probs, caches, strict=True):
        mixed = jnp.dot(prob, cache[:, :lat], preferred_element_type=jnp.float32)
        out_ref[at : at + pair] = mixed.astype(jnp.bfloat16).reshape(pair, heads, lat)


def attend_piece(lengths, queries, latent_cache, lat, piece, count, out, after):
    total, heads, wide = queries.shape
    slots = latent_cache.shape[1]

    def rows(middle, last):
        return pl.BlockSpec((count, middle, last), lambda i, n: (piece, 0, 0))

    extra = ([] if out is None else [out]) + list(after)
    return pl.pallas_call(
        functools.partial(attend_kernel, base=piece * count, pair=2),
        grid_spec=pltpu.PrefetchScalarGridSpec(
            num_scalar_prefetch=1,
            grid=(1,),
            in_specs=[rows(heads, wide), rows(slots, wide)]
            + [pl.BlockSpec(memory_space=pl.ANY)] * len(extra),
            out_specs=[rows(heads, lat), pl.BlockSpec((8, LANES), lambda i, n: (0, 0))],
        ),
        out_shape=[
            jax.ShapeDtypeStruct((total, heads, lat), jnp.bfloat16),
            jax.ShapeDtypeStruct((8, LANES), jnp.float32),
        ],
        input_output_aliases={} if out is None else {3: 0},
        compiler_params=pltpu.CompilerParams(vmem_limit_bytes=16 << 20),
        cost_estimate=pl.CostEstimate(
            flops=2 * count * heads * slots * (wide + lat),
            bytes_accessed=2 * count * (heads * (wide + lat) + slots * wide),
            transcendentals=count * heads * slots,
        ),
        name="attend",
    )(lengths, queries, latent_cache, *extra)


def expert_kernel(expert_ref, own_ref, other_ref, gate_ref, up_ref, down_ref, *rest):
    own_out, other_out = rest[-2:]
    rows, width = own_out.shape
    x = jnp.concatenate([own_ref[:, :width], other_ref[:, :width]], axis=0)
    gate = jnp.dot(x, gate_ref[...], preferred_element_type=jnp.float32)
    up = jnp.dot(x, up_ref[...], preferred_element_type=jnp.float32)
    hidden = (gate / (1.0 + jnp.exp(-gate)) * up).astype(jnp.bfloat16)
    down = jnp.dot(hidden, down_ref[...], preferred_element_type=jnp.float32)
    lane = lax.broadcasted_iota(jnp.int32, (rows, LANES), 1)
    for at, source, out in ((0, own_ref, own_out), (rows, other_ref, other_out)):
        route = source[:, width:].astype(jnp.float32)
        weight = jnp.sum(jnp.where(lane == expert_ref[0], route, 0.0), axis=1, keepdims=True)
        out[...] = (weight * down[at : at + rows]).astype(jnp.bfloat16)


def run_experts(expert, own, other, gate, up, down, after=()):
    rows, wide = own.shape
    width, hidden = gate.shape

    def whole(shape):
        return pl.BlockSpec(shape, lambda i, e: (0, 0))

    return pl.pallas_call(
        expert_kernel,
        grid_spec=pltpu.PrefetchScalarGridSpec(
            num_scalar_prefetch=1,
            grid=(1,),
            in_specs=[
                whole((rows, wide)),
                whole((rows, wide)),
                whole((width, hidden)),
                whole((width, hidden)),
                whole((hidden, width)),
            ]
            + [pl.BlockSpec(memory_space=pl.ANY)] * len(after),
            out_specs=[whole((rows, width)), whole((rows, width))],
        ),
        out_shape=[jax.ShapeDtypeStruct((rows, width), jnp.bfloat16)] * 2,
        compiler_params=pltpu.CompilerParams(vmem_limit_bytes=16 << 20),
        cost_estimate=pl.CostEstimate(
            flops=12 * rows * width * hidden,
            bytes_accessed=6 * width * hidden,
            transcendentals=2 * rows * hidden,
        ),
        name="expert_half",
    )(expert, own, other, gate, up, down, *after)


def ring_order(count):
    if count == 8:
        return [0, 2, 4, 6, 7, 5, 3, 1]
    return list(range(count))


def on_device(
    tokens, expert_ids, combine_weights, w_gate, w_up, w_down, queries, latent_cache, cache_lengths
):
    local_count = lax.axis_size("local")
    rows, width = tokens.shape
    part = rows // 2
    node = lax.axis_index("node")
    order = ring_order(local_count)
    hops, hops_out = [], []
    for i in range(local_count):
        here, there = order[i], order[(i + 1) % local_count]
        hops += [(here, there), (local_count + there, local_count + here)]
        hops_out += [(here, local_count + there), (local_count + there, here)]
    expert = ((node * local_count + lax.axis_index("local")) // 2).astype(jnp.int32).reshape(1)

    def onward(a, pairs=hops):
        return lax.ppermute(a, ("node", "local"), pairs)

    def across(a):
        return lax.ppermute(a, "node", [(0, 1), (1, 0)])

    matches = expert_ids[:, :, None] == jnp.arange(LANES, dtype=jnp.int32)[None, None, :]
    route = jnp.sum(
        jnp.where(matches, combine_weights[:, :, None], jnp.zeros((), jnp.bfloat16)), axis=1
    )
    first = node == 0

    def halves(a):
        return jnp.where(first, a[:part], a[part:]), jnp.where(first, a[part:], a[:part])

    kept, given = [
        jnp.concatenate(pair, axis=1) for pair in zip(halves(tokens), halves(route), strict=True)
    ]
    swapped = across(given)
    block = jnp.concatenate([kept, swapped], axis=0)
    mine = jnp.concatenate([tokens, lax.optimization_barrier((route, block))[0]], axis=1)
    gate, up, down = w_gate[0], w_up[0], w_down[0]
    own, other = run_experts(expert, mine, across(mine), gate, up, down)
    own_sums, other_sums = [own], [across(other)]
    after = (own,)
    attn_latent, done = None, None
    for k in range(1, local_count):
        block = onward(block)
        if k == 1:
            block = lax.optimization_barrier((block, own))[0]
        own, other = run_experts(expert, block, across(block), gate, up, down, after)
        own_sums.append(own)
        other_sums.append(across(other))
        after = ()
        if done is not None:
            after, done = (done,), None
        if k <= PIECES:
            attn_latent, done = attend_piece(
                cache_lengths,
                queries,
                latent_cache,
                LAT,
                k - 1,
                queries.shape[0] // PIECES,
                attn_latent,
                (own,),
            )

    def chip_sum(k):
        return own_sums[k].astype(jnp.float32) + other_sums[k].astype(jnp.float32)

    running = chip_sum(1).astype(jnp.bfloat16)
    for k in range(2, local_count - 1):
        running = (chip_sum(k) + onward(running).astype(jnp.float32)).astype(jnp.bfloat16)
    total = chip_sum(local_count - 1) + onward(running).astype(jnp.float32)
    same = onward(total[:part].astype(jnp.bfloat16))
    cross = onward(total[part:].astype(jnp.bfloat16), hops_out)
    arrived = jnp.where(
        first, jnp.concatenate([same, cross], axis=0), jnp.concatenate([cross, same], axis=0)
    )
    moe_out = (chip_sum(0) + arrived.astype(jnp.float32)).astype(jnp.bfloat16)

    return (moe_out, attn_latent)


def solution(mesh):
    in_specs = (
        P(("replica", "node", "local"), None),
        P(("replica", "node", "local"), None),
        P(("replica", "node", "local"), None),
        P(("node", "local"), None, None),
        P(("node", "local"), None, None),
        P(("node", "local"), None, None),
        P(("replica", "node", "local"), None, None),
        P(("replica", "node", "local"), None, None),
        P(("replica", "node", "local")),
    )
    out_specs = (P(("replica", "node", "local"), None), P(("replica", "node", "local"), None, None))
    return jax.shard_map(
        on_device, mesh=mesh, in_specs=in_specs, out_specs=out_specs, check_vma=False
    )
```

```python
import functools

import jax
import jax.numpy as jnp
from jax import lax
from jax.experimental import pallas as pl
from jax.experimental.pallas import tpu as pltpu
from jax.sharding import PartitionSpec as P

LAT = 512
SOFTMAX_SCALE = 192.0 ** (-0.5)
LANES = 128
PIECES = 4


def attend_kernel(len_ref, q_ref, c_ref, *rest, base, pair):
    done_ref = rest[-1]
    done_ref[...] = jnp.zeros_like(done_ref)
    out_ref = rest[-2]
    step, heads, wide = q_ref.shape
    slots = c_ref.shape[1]
    lat = out_ref.shape[2]
    row = lax.broadcasted_iota(jnp.int32, (pair * heads, pair * slots), 0) // heads
    col = lax.broadcasted_iota(jnp.int32, (pair * heads, pair * slots), 1)
    place = jnp.where(col // slots == row, col % slots, slots)
    which = lax.broadcasted_iota(jnp.int32, (pair * heads, 1), 0) // heads
    groups = range(0, step, pair)
    caches = [c_ref[at : at + pair].reshape(pair * slots, wide) for at in groups]
    scores = [
        lax.dot_general(
            q_ref[at : at + pair].reshape(pair * heads, wide),
            cache,
            (((1,), (1,)), ((), ())),
            preferred_element_type=jnp.float32,
        )
        for at, cache in zip(groups, caches, strict=True)
    ]
    probs = []
    for at, score in zip(groups, scores, strict=True):
        live = jnp.full((pair * heads, 1), len_ref[base + at], jnp.int32)
        for j in range(1, pair):
            live = jnp.where(which == j, len_ref[base + at + j], live)
        score = jnp.where(place < live, score * SOFTMAX_SCALE, -1e30)
        terms = jnp.exp(score - jnp.max(score, axis=1, keepdims=True))
        probs.append((terms * (1.0 / jnp.sum(terms, axis=1, keepdims=True))).astype(jnp.bfloat16))
    for at, prob, cache in zip(groups, probs, caches, strict=True):
        mixed = jnp.dot(prob, cache[:, :lat], preferred_element_type=jnp.float32)
        out_ref[at : at + pair] = mixed.astype(jnp.bfloat16).reshape(pair, heads, lat)


def attend_piece(lengths, queries, latent_cache, lat, piece, count, out, after):
    total, heads, wide = queries.shape
    slots = latent_cache.shape[1]

    def rows(middle, last):
        return pl.BlockSpec((count, middle, last), lambda i, n: (piece, 0, 0))

    extra = ([] if out is None else [out]) + list(after)
    return pl.pallas_call(
        functools.partial(attend_kernel, base=piece * count, pair=2),
        grid_spec=pltpu.PrefetchScalarGridSpec(
            num_scalar_prefetch=1,
            grid=(1,),
            in_specs=[rows(heads, wide), rows(slots, wide)]
            + [pl.BlockSpec(memory_space=pl.ANY)] * len(extra),
            out_specs=[rows(heads, lat), pl.BlockSpec((8, LANES), lambda i, n: (0, 0))],
        ),
        out_shape=[
            jax.ShapeDtypeStruct((total, heads, lat), jnp.bfloat16),
            jax.ShapeDtypeStruct((8, LANES), jnp.float32),
        ],
        input_output_aliases={} if out is None else {3: 0},
        compiler_params=pltpu.CompilerParams(vmem_limit_bytes=16 << 20),
        cost_estimate=pl.CostEstimate(
            flops=2 * count * heads * slots * (wide + lat),
            bytes_accessed=2 * count * (heads * (wide + lat) + slots * wide),
            transcendentals=count * heads * slots,
        ),
        name="attend",
    )(lengths, queries, latent_cache, *extra)


def expert_kernel(expert_ref, *refs, own_parts, parts):
    sources = refs[:parts]
    gate_ref, up_ref, down_ref = refs[parts : parts + 3]
    outs = refs[-2:]
    width = outs[0].shape[1]
    x = jnp.concatenate([source[:, :width] for source in sources], axis=0)
    gate = jnp.dot(x, gate_ref[...], preferred_element_type=jnp.float32)
    up = jnp.dot(x, up_ref[...], preferred_element_type=jnp.float32)
    hidden = (gate / (1.0 + jnp.exp(-gate)) * up).astype(jnp.bfloat16)
    down = jnp.dot(hidden, down_ref[...], preferred_element_type=jnp.float32)
    at = 0
    for i, source in enumerate(sources):
        rows = source.shape[0]
        lane = lax.broadcasted_iota(jnp.int32, (rows, LANES), 1)
        route = source[:, width:].astype(jnp.float32)
        weight = jnp.sum(jnp.where(lane == expert_ref[0], route, 0.0), axis=1, keepdims=True)
        out = outs[0] if i < own_parts else outs[1]
        to = at if i < own_parts else at - outs[0].shape[0]
        out[to : to + rows] = (weight * down[at : at + rows]).astype(jnp.bfloat16)
        at += rows


def run_experts(expert, own, other, gate, up, down, after=()):
    counts = [sum(part.shape[0] for part in parts) for parts in (own, other)]
    width, hidden = gate.shape
    inputs = (*own, *other, gate, up, down)
    return pl.pallas_call(
        functools.partial(
            expert_kernel, own_parts=len(own), parts=len(own) + len(other)
        ),
        grid_spec=pltpu.PrefetchScalarGridSpec(
            num_scalar_prefetch=1,
            grid=(1,),
            in_specs=[pl.BlockSpec(a.shape, lambda i, e: (0, 0)) for a in inputs]
            + [pl.BlockSpec(memory_space=pl.ANY)] * len(after),
            out_specs=[pl.BlockSpec((count, width), lambda i, e: (0, 0)) for count in counts],
        ),
        out_shape=[jax.ShapeDtypeStruct((count, width), jnp.bfloat16) for count in counts],
        compiler_params=pltpu.CompilerParams(vmem_limit_bytes=16 << 20),
        cost_estimate=pl.CostEstimate(
            flops=6 * sum(counts) * width * hidden,
            bytes_accessed=6 * width * hidden,
            transcendentals=sum(counts) * hidden,
        ),
        name="expert_half",
    )(expert, *inputs, *after)


def join_kernel(first_ref, second_ref, out_ref):
    rows = first_ref.shape[0]
    out_ref[:rows] = first_ref[...]
    out_ref[rows:] = second_ref[...]


def join(first, second):
    rows, width = first.shape
    return pl.pallas_call(
        join_kernel,
        grid=(1,),
        in_specs=[pl.BlockSpec((rows, width), lambda i: (0, 0))] * 2,
        out_specs=pl.BlockSpec((2 * rows, width), lambda i: (0, 0)),
        out_shape=jax.ShapeDtypeStruct((2 * rows, width), first.dtype),
        compiler_params=pltpu.CompilerParams(vmem_limit_bytes=16 << 20),
        name="join",
    )(first, second)


def ring_order(count):
    if count == 8:
        return [0, 2, 4, 6, 7, 5, 3, 1]
    return list(range(count))


def on_device(
    tokens, expert_ids, combine_weights, w_gate, w_up, w_down, queries, latent_cache, cache_lengths
):
    local_count = lax.axis_size("local")
    rows, width = tokens.shape
    part = rows // 2
    node = lax.axis_index("node")
    order = ring_order(local_count)
    hops, hops_out = [], []
    for i in range(local_count):
        here, there = order[i], order[(i + 1) % local_count]
        hops += [(here, there), (local_count + there, local_count + here)]
        hops_out += [(here, local_count + there), (local_count + there, here)]
    expert = ((node * local_count + lax.axis_index("local")) // 2).astype(jnp.int32).reshape(1)

    def onward(a, pairs=hops):
        return lax.ppermute(a, ("node", "local"), pairs)

    def across(a):
        return lax.ppermute(a, "node", [(0, 1), (1, 0)])

    def chip_sum(a, b):
        return a.astype(jnp.float32) + b.astype(jnp.float32)

    matches = expert_ids[:, :, None] == jnp.arange(LANES, dtype=jnp.int32)[None, None, :]
    route = jnp.sum(
        jnp.where(matches, combine_weights[:, :, None], jnp.zeros((), jnp.bfloat16)), axis=1
    )
    first = node == 0

    def halves(a):
        return jnp.where(first, a[:part], a[part:]), jnp.where(first, a[part:], a[:part])

    kept, given = [
        jnp.concatenate(pair, axis=1) for pair in zip(halves(tokens), halves(route), strict=True)
    ]
    swapped = across(given)
    gate, up, down = w_gate[0], w_up[0], w_down[0]
    block = join(onward(kept), onward(swapped))
    own, other = run_experts(
        expert, (kept, given), (across(kept), swapped), gate, up, down
    )
    block = lax.optimization_barrier((block, own))[0]
    mine_sum = chip_sum(own, across(other))
    after = (own,)
    attn_latent, done = None, None
    for k in range(1, local_count):
        if k > 1:
            block = onward(block)
        own, other = run_experts(expert, (block,), (across(block),), gate, up, down, after)
        total = chip_sum(own, across(other))
        if k > 1:
            total += onward(running).astype(jnp.float32)
        running = total.astype(jnp.bfloat16)
        after = ()
        if done is not None:
            after, done = (done,), None
        if k <= PIECES:
            attn_latent, done = attend_piece(
                cache_lengths,
                queries,
                latent_cache,
                LAT,
                k - 1,
                queries.shape[0] // PIECES,
                attn_latent,
                (own,),
            )

    mine_sum = lax.optimization_barrier(
        jnp.where(first, mine_sum, jnp.concatenate([mine_sum[part:], mine_sum[:part]], axis=0))
    )
    same, cross = onward(running[:part]), onward(running[part:], hops_out)
    arrived = jnp.where(
        first, jnp.concatenate([same, cross], axis=0), jnp.concatenate([cross, same], axis=0)
    )
    moe_out = (mine_sum + arrived.astype(jnp.float32)).astype(jnp.bfloat16)

    return (moe_out, attn_latent)


def solution(mesh):
    in_specs = (
        P(("replica", "node", "local"), None),
        P(("replica", "node", "local"), None),
        P(("replica", "node", "local"), None),
        P(("node", "local"), None, None),
        P(("node", "local"), None, None),
        P(("node", "local"), None, None),
        P(("replica", "node", "local"), None, None),
        P(("replica", "node", "local"), None, None),
        P(("replica", "node", "local")),
    )
    out_specs = (P(("replica", "node", "local"), None), P(("replica", "node", "local"), None, None))
    return jax.shard_map(
        on_device, mesh=mesh, in_specs=in_specs, out_specs=out_specs, check_vma=False
    )
```

```python
import functools

import jax
import jax.numpy as jnp
from jax import lax
from jax.experimental import pallas as pl
from jax.experimental.pallas import tpu as pltpu
from jax.sharding import PartitionSpec as P

LAT = 512
SOFTMAX_SCALE = 192.0 ** (-0.5)
LANES = 128
PIECES = 4


def attend_kernel(len_ref, q_ref, c_ref, *rest, base, pair):
    done_ref = rest[-1]
    done_ref[...] = jnp.zeros_like(done_ref)
    out_ref = rest[-2]
    step, heads, wide = q_ref.shape
    slots = c_ref.shape[1]
    lat = out_ref.shape[2]
    row = lax.broadcasted_iota(jnp.int32, (pair * heads, pair * slots), 0) // heads
    col = lax.broadcasted_iota(jnp.int32, (pair * heads, pair * slots), 1)
    place = jnp.where(col // slots == row, col % slots, slots)
    which = lax.broadcasted_iota(jnp.int32, (pair * heads, 1), 0) // heads
    groups = range(0, step, pair)
    caches = [c_ref[at : at + pair].reshape(pair * slots, wide) for at in groups]
    scores = [
        lax.dot_general(
            q_ref[at : at + pair].reshape(pair * heads, wide),
            cache,
            (((1,), (1,)), ((), ())),
            preferred_element_type=jnp.float32,
        )
        for at, cache in zip(groups, caches, strict=True)
    ]
    probs = []
    for at, score in zip(groups, scores, strict=True):
        live = jnp.full((pair * heads, 1), len_ref[base + at], jnp.int32)
        for j in range(1, pair):
            live = jnp.where(which == j, len_ref[base + at + j], live)
        score = jnp.where(place < live, score * SOFTMAX_SCALE, -1e30)
        terms = jnp.exp(score - jnp.max(score, axis=1, keepdims=True))
        probs.append((terms * (1.0 / jnp.sum(terms, axis=1, keepdims=True))).astype(jnp.bfloat16))
    for at, prob, cache in zip(groups, probs, caches, strict=True):
        mixed = jnp.dot(prob, cache[:, :lat], preferred_element_type=jnp.float32)
        out_ref[at : at + pair] = mixed.astype(jnp.bfloat16).reshape(pair, heads, lat)


def attend_piece(lengths, queries, latent_cache, lat, piece, count, out, after):
    total, heads, wide = queries.shape
    slots = latent_cache.shape[1]

    def rows(middle, last):
        return pl.BlockSpec((count, middle, last), lambda i, n: (piece, 0, 0))

    extra = ([] if out is None else [out]) + list(after)
    return pl.pallas_call(
        functools.partial(attend_kernel, base=piece * count, pair=2),
        grid_spec=pltpu.PrefetchScalarGridSpec(
            num_scalar_prefetch=1,
            grid=(1,),
            in_specs=[rows(heads, wide), rows(slots, wide)]
            + [pl.BlockSpec(memory_space=pl.ANY)] * len(extra),
            out_specs=[rows(heads, lat), pl.BlockSpec((8, LANES), lambda i, n: (0, 0))],
        ),
        out_shape=[
            jax.ShapeDtypeStruct((total, heads, lat), jnp.bfloat16),
            jax.ShapeDtypeStruct((8, LANES), jnp.float32),
        ],
        input_output_aliases={} if out is None else {3: 0},
        compiler_params=pltpu.CompilerParams(vmem_limit_bytes=16 << 20),
        cost_estimate=pl.CostEstimate(
            flops=2 * count * heads * slots * (wide + lat),
            bytes_accessed=2 * count * (heads * (wide + lat) + slots * wide),
            transcendentals=count * heads * slots,
        ),
        name="attend",
    )(lengths, queries, latent_cache, *extra)


def expert_kernel(expert_ref, *refs, own_parts, parts):
    sources = refs[:parts]
    gate_ref, up_ref, down_ref = refs[parts : parts + 3]
    outs = refs[-2:]
    width = outs[0].shape[1]
    x = jnp.concatenate([source[:, :width] for source in sources], axis=0)
    gate = jnp.dot(x, gate_ref[...], preferred_element_type=jnp.float32)
    up = jnp.dot(x, up_ref[...], preferred_element_type=jnp.float32)
    hidden = (gate / (1.0 + jnp.exp(-gate)) * up).astype(jnp.bfloat16)
    down = jnp.dot(hidden, down_ref[...], preferred_element_type=jnp.float32)
    at = 0
    for i, source in enumerate(sources):
        rows = source.shape[0]
        lane = lax.broadcasted_iota(jnp.int32, (rows, LANES), 1)
        route = source[:, width:].astype(jnp.float32)
        weight = jnp.sum(jnp.where(lane == expert_ref[0], route, 0.0), axis=1, keepdims=True)
        out = outs[0] if i < own_parts else outs[1]
        to = at if i < own_parts else at - outs[0].shape[0]
        out[to : to + rows] = (weight * down[at : at + rows]).astype(jnp.bfloat16)
        at += rows


def run_experts(expert, own, other, gate, up, down, after=()):
    counts = [sum(part.shape[0] for part in parts) for parts in (own, other)]
    width, hidden = gate.shape
    inputs = (*own, *other, gate, up, down)
    return pl.pallas_call(
        functools.partial(
            expert_kernel, own_parts=len(own), parts=len(own) + len(other)
        ),
        grid_spec=pltpu.PrefetchScalarGridSpec(
            num_scalar_prefetch=1,
            grid=(1,),
            in_specs=[pl.BlockSpec(a.shape, lambda i, e: (0, 0)) for a in inputs]
            + [pl.BlockSpec(memory_space=pl.ANY)] * len(after),
            out_specs=[pl.BlockSpec((count, width), lambda i, e: (0, 0)) for count in counts],
        ),
        out_shape=[jax.ShapeDtypeStruct((count, width), jnp.bfloat16) for count in counts],
        compiler_params=pltpu.CompilerParams(vmem_limit_bytes=16 << 20),
        cost_estimate=pl.CostEstimate(
            flops=6 * sum(counts) * width * hidden,
            bytes_accessed=6 * width * hidden,
            transcendentals=sum(counts) * hidden,
        ),
        name="expert_half",
    )(expert, *inputs, *after)


def load_kernel(*refs, count):
    sources, targets, sems = refs[:count], refs[-count - 1 : -1], refs[-1]
    copies = [
        pltpu.make_async_copy(sources[i].at[0], targets[i], sems.at[i]) for i in range(count)
    ]
    for copy in copies:
        copy.start()
    for copy in copies:
        copy.wait()


def load_weights(weights, after):
    count = len(weights)
    anywhere = pl.BlockSpec(memory_space=pl.ANY)
    return pl.pallas_call(
        functools.partial(load_kernel, count=count),
        in_specs=[anywhere] * (count + len(after)),
        out_specs=[anywhere] * count,
        out_shape=[jax.ShapeDtypeStruct(w.shape[1:], w.dtype) for w in weights],
        scratch_shapes=[pltpu.SemaphoreType.DMA((count,))],
        compiler_params=pltpu.CompilerParams(vmem_limit_bytes=41 << 20),
        cost_estimate=pl.CostEstimate(
            flops=0, bytes_accessed=2 * sum(w.size for w in weights), transcendentals=0
        ),
        name="load_weights",
    )(*weights, *after)


def join_kernel(first_ref, second_ref, out_ref):
    rows = first_ref.shape[0]
    out_ref[:rows] = first_ref[...]
    out_ref[rows:] = second_ref[...]


def join(first, second):
    rows, width = first.shape
    return pl.pallas_call(
        join_kernel,
        grid=(1,),
        in_specs=[pl.BlockSpec((rows, width), lambda i: (0, 0))] * 2,
        out_specs=pl.BlockSpec((2 * rows, width), lambda i: (0, 0)),
        out_shape=jax.ShapeDtypeStruct((2 * rows, width), first.dtype),
        compiler_params=pltpu.CompilerParams(vmem_limit_bytes=16 << 20),
        name="join",
    )(first, second)


def ring_order(count):
    if count == 8:
        return [0, 2, 4, 6, 7, 5, 3, 1]
    return list(range(count))


def on_device(
    tokens, expert_ids, combine_weights, w_gate, w_up, w_down, queries, latent_cache, cache_lengths
):
    local_count = lax.axis_size("local")
    rows, width = tokens.shape
    part = rows // 2
    node = lax.axis_index("node")
    order = ring_order(local_count)
    hops, hops_out = [], []
    for i in range(local_count):
        here, there = order[i], order[(i + 1) % local_count]
        hops += [(here, there), (local_count + there, local_count + here)]
        hops_out += [(here, local_count + there), (local_count + there, here)]
    expert = ((node * local_count + lax.axis_index("local")) // 2).astype(jnp.int32).reshape(1)

    def onward(a, pairs=hops):
        return lax.ppermute(a, ("node", "local"), pairs)

    def across(a):
        return lax.ppermute(a, "node", [(0, 1), (1, 0)])

    def chip_sum(a, b):
        return a.astype(jnp.float32) + b.astype(jnp.float32)

    matches = expert_ids[:, :, None] == jnp.arange(LANES, dtype=jnp.int32)[None, None, :]
    route = jnp.sum(
        jnp.where(matches, combine_weights[:, :, None], jnp.zeros((), jnp.bfloat16)), axis=1
    )
    first = node == 0

    def halves(a):
        return jnp.where(first, a[:part], a[part:]), jnp.where(first, a[part:], a[:part])

    kept, given = [
        jnp.concatenate(pair, axis=1) for pair in zip(halves(tokens), halves(route), strict=True)
    ]
    swapped = across(given)
    gate, up, down = load_weights((w_gate, w_up, w_down), (kept,))
    block = join(onward(kept), onward(swapped))
    own, other = run_experts(
        expert, (kept, given), (across(kept), swapped), gate, up, down
    )
    block = lax.optimization_barrier((block, own))[0]
    mine_sum = chip_sum(own, across(other))
    after = (own,)
    attn_latent, done = None, None
    for k in range(1, local_count):
        if k > 1:
            block = onward(block)
        own, other = run_experts(expert, (block,), (across(block),), gate, up, down, after)
        total = chip_sum(own, across(other))
        if k > 1:
            total += onward(running).astype(jnp.float32)
        running = total.astype(jnp.bfloat16)
        after = ()
        if done is not None:
            after, done = (done,), None
        if k <= PIECES:
            attn_latent, done = attend_piece(
                cache_lengths,
                queries,
                latent_cache,
                LAT,
                k - 1,
                queries.shape[0] // PIECES,
                attn_latent,
                (own,),
            )

    mine_sum = lax.optimization_barrier(
        jnp.where(first, mine_sum, jnp.concatenate([mine_sum[part:], mine_sum[:part]], axis=0))
    )
    same, cross = onward(running[:part]), onward(running[part:], hops_out)
    arrived = jnp.where(
        first, jnp.concatenate([same, cross], axis=0), jnp.concatenate([cross, same], axis=0)
    )
    moe_out = (mine_sum + arrived.astype(jnp.float32)).astype(jnp.bfloat16)

    return (moe_out, attn_latent)


def solution(mesh):
    in_specs = (
        P(("replica", "node", "local"), None),
        P(("replica", "node", "local"), None),
        P(("replica", "node", "local"), None),
        P(("node", "local"), None, None),
        P(("node", "local"), None, None),
        P(("node", "local"), None, None),
        P(("replica", "node", "local"), None, None),
        P(("replica", "node", "local"), None, None),
        P(("replica", "node", "local")),
    )
    out_specs = (P(("replica", "node", "local"), None), P(("replica", "node", "local"), None, None))
    return jax.shard_map(
        on_device, mesh=mesh, in_specs=in_specs, out_specs=out_specs, check_vma=False
    )
```

```python
import functools

import jax
import jax.numpy as jnp
from jax import lax
from jax.experimental import pallas as pl
from jax.experimental.pallas import tpu as pltpu
from jax.sharding import PartitionSpec as P

LAT = 512
SOFTMAX_SCALE = 192.0 ** (-0.5)
LANES = 128
PIECES = 4


def attend_kernel(len_ref, q_ref, c_ref, *rest, base, pair):
    done_ref = rest[-1]
    done_ref[...] = jnp.zeros_like(done_ref)
    out_ref = rest[-2]
    step, heads, wide = q_ref.shape
    slots = c_ref.shape[1]
    lat = out_ref.shape[2]
    row = lax.broadcasted_iota(jnp.int32, (pair * heads, pair * slots), 0) // heads
    col = lax.broadcasted_iota(jnp.int32, (pair * heads, pair * slots), 1)
    place = jnp.where(col // slots == row, col % slots, slots)
    which = lax.broadcasted_iota(jnp.int32, (pair * heads, 1), 0) // heads
    groups = range(0, step, pair)
    caches = [c_ref[at : at + pair].reshape(pair * slots, wide) for at in groups]
    scores = [
        lax.dot_general(
            q_ref[at : at + pair].reshape(pair * heads, wide),
            cache,
            (((1,), (1,)), ((), ())),
            preferred_element_type=jnp.float32,
        )
        for at, cache in zip(groups, caches, strict=True)
    ]
    probs = []
    for at, score in zip(groups, scores, strict=True):
        live = jnp.full((pair * heads, 1), len_ref[base + at], jnp.int32)
        for j in range(1, pair):
            live = jnp.where(which == j, len_ref[base + at + j], live)
        score = jnp.where(place < live, score * SOFTMAX_SCALE, -1e30)
        terms = jnp.exp(score - jnp.max(score, axis=1, keepdims=True))
        probs.append((terms * (1.0 / jnp.sum(terms, axis=1, keepdims=True))).astype(jnp.bfloat16))
    for at, prob, cache in zip(groups, probs, caches, strict=True):
        mixed = jnp.dot(prob, cache[:, :lat], preferred_element_type=jnp.float32)
        out_ref[at : at + pair] = mixed.astype(jnp.bfloat16).reshape(pair, heads, lat)


def attend_piece(lengths, queries, latent_cache, lat, piece, count, out, after):
    total, heads, wide = queries.shape
    slots = latent_cache.shape[1]

    def rows(middle, last):
        return pl.BlockSpec((count, middle, last), lambda i, n: (piece, 0, 0))

    extra = ([] if out is None else [out]) + list(after)
    return pl.pallas_call(
        functools.partial(attend_kernel, base=piece * count, pair=2),
        grid_spec=pltpu.PrefetchScalarGridSpec(
            num_scalar_prefetch=1,
            grid=(1,),
            in_specs=[rows(heads, wide), rows(slots, wide)]
            + [pl.BlockSpec(memory_space=pl.ANY)] * len(extra),
            out_specs=[rows(heads, lat), pl.BlockSpec((8, LANES), lambda i, n: (0, 0))],
        ),
        out_shape=[
            jax.ShapeDtypeStruct((total, heads, lat), jnp.bfloat16),
            jax.ShapeDtypeStruct((8, LANES), jnp.float32),
        ],
        input_output_aliases={} if out is None else {3: 0},
        compiler_params=pltpu.CompilerParams(vmem_limit_bytes=16 << 20),
        cost_estimate=pl.CostEstimate(
            flops=2 * count * heads * slots * (wide + lat),
            bytes_accessed=2 * count * (heads * (wide + lat) + slots * wide),
            transcendentals=count * heads * slots,
        ),
        name="attend",
    )(lengths, queries, latent_cache, *extra)


def expert_kernel(expert_ref, *refs, own_parts, parts):
    sources = refs[:parts]
    gate_ref, up_ref, down_ref = refs[parts : parts + 3]
    outs = refs[-2:]
    width = outs[0].shape[1]
    x = jnp.concatenate([source[:, :width] for source in sources], axis=0)
    gate = jnp.dot(x, gate_ref[...], preferred_element_type=jnp.float32)
    up = jnp.dot(x, up_ref[...], preferred_element_type=jnp.float32)
    hidden = (gate / (1.0 + jnp.exp(-gate)) * up).astype(jnp.bfloat16)
    down = jnp.dot(hidden, down_ref[...], preferred_element_type=jnp.float32)
    at = 0
    for i, source in enumerate(sources):
        rows = source.shape[0]
        lane = lax.broadcasted_iota(jnp.int32, (rows, LANES), 1)
        route = source[:, width:].astype(jnp.float32)
        weight = jnp.sum(jnp.where(lane == expert_ref[0], route, 0.0), axis=1, keepdims=True)
        out = outs[0] if i < own_parts else outs[1]
        to = at if i < own_parts else at - outs[0].shape[0]
        out[to : to + rows] = (weight * down[at : at + rows]).astype(jnp.bfloat16)
        at += rows


def run_experts(expert, own, other, gate, up, down, after=()):
    counts = [sum(part.shape[0] for part in parts) for parts in (own, other)]
    width, hidden = gate.shape
    inputs = (*own, *other, gate, up, down)
    return pl.pallas_call(
        functools.partial(
            expert_kernel, own_parts=len(own), parts=len(own) + len(other)
        ),
        grid_spec=pltpu.PrefetchScalarGridSpec(
            num_scalar_prefetch=1,
            grid=(1,),
            in_specs=[pl.BlockSpec(a.shape, lambda i, e: (0, 0)) for a in inputs]
            + [pl.BlockSpec(memory_space=pl.ANY)] * len(after),
            out_specs=[pl.BlockSpec((count, width), lambda i, e: (0, 0)) for count in counts],
        ),
        out_shape=[jax.ShapeDtypeStruct((count, width), jnp.bfloat16) for count in counts],
        compiler_params=pltpu.CompilerParams(vmem_limit_bytes=16 << 20),
        cost_estimate=pl.CostEstimate(
            flops=6 * sum(counts) * width * hidden,
            bytes_accessed=6 * width * hidden,
            transcendentals=sum(counts) * hidden,
        ),
        name="expert_half",
    )(expert, *inputs, *after)


def load_kernel(*refs, count):
    sources, targets, sems = refs[:count], refs[-count - 1 : -1], refs[-1]
    copies = [
        pltpu.make_async_copy(sources[i].at[0], targets[i], sems.at[i]) for i in range(count)
    ]
    for copy in copies:
        copy.start()
    for copy in copies:
        copy.wait()


def load_weights(weights, after):
    count = len(weights)
    anywhere = pl.BlockSpec(memory_space=pl.ANY)
    return pl.pallas_call(
        functools.partial(load_kernel, count=count),
        in_specs=[anywhere] * (count + len(after)),
        out_specs=[anywhere] * count,
        out_shape=[jax.ShapeDtypeStruct(w.shape[1:], w.dtype) for w in weights],
        scratch_shapes=[pltpu.SemaphoreType.DMA((count,))],
        compiler_params=pltpu.CompilerParams(vmem_limit_bytes=41 << 20),
        cost_estimate=pl.CostEstimate(
            flops=0, bytes_accessed=2 * sum(w.size for w in weights), transcendentals=0
        ),
        name="load_weights",
    )(*weights, *after)


def join_kernel(first_ref, second_ref, out_ref):
    rows = first_ref.shape[0]
    out_ref[:rows] = first_ref[...]
    out_ref[rows:] = second_ref[...]


def join(first, second):
    rows, width = first.shape
    return pl.pallas_call(
        join_kernel,
        grid=(1,),
        in_specs=[pl.BlockSpec((rows, width), lambda i: (0, 0))] * 2,
        out_specs=pl.BlockSpec((2 * rows, width), lambda i: (0, 0)),
        out_shape=jax.ShapeDtypeStruct((2 * rows, width), first.dtype),
        compiler_params=pltpu.CompilerParams(vmem_limit_bytes=16 << 20),
        name="join",
    )(first, second)


def ring_order(count):
    if count == 8:
        return [0, 2, 4, 6, 7, 5, 3, 1]
    return list(range(count))


def on_device(
    tokens, expert_ids, combine_weights, w_gate, w_up, w_down, queries, latent_cache, cache_lengths
):
    local_count = lax.axis_size("local")
    rows, width = tokens.shape
    part = rows // 2
    node = lax.axis_index("node")
    order = ring_order(local_count)
    hops, hops_out = [], []
    for i in range(local_count):
        here, there = order[i], order[(i + 1) % local_count]
        hops += [(here, there), (local_count + there, local_count + here)]
        hops_out += [(here, local_count + there), (local_count + there, here)]
    expert = ((node * local_count + lax.axis_index("local")) // 2).astype(jnp.int32).reshape(1)

    def onward(a, pairs=hops):
        return lax.ppermute(a, ("node", "local"), pairs)

    def across(a):
        return lax.ppermute(a, "node", [(0, 1), (1, 0)])

    def chip_sum(a, b):
        return a.astype(jnp.float32) + b.astype(jnp.float32)

    matches = expert_ids[:, :, None] == jnp.arange(LANES, dtype=jnp.int32)[None, None, :]
    route = jnp.sum(
        jnp.where(matches, combine_weights[:, :, None], jnp.zeros((), jnp.bfloat16)), axis=1
    )
    first = node == 0

    def halves(a):
        return jnp.where(first, a[:part], a[part:]), jnp.where(first, a[part:], a[:part])

    kept, given = [
        jnp.concatenate(pair, axis=1) for pair in zip(halves(tokens), halves(route), strict=True)
    ]
    swapped = across(given)
    gate, up, down = load_weights((w_gate, w_up, w_down), (kept,))
    block = join(onward(kept), onward(swapped))
    own, other = run_experts(
        expert, (kept, given), (across(kept), swapped), gate, up, down
    )
    block = lax.optimization_barrier((block, own))[0]
    mine_sum = chip_sum(own, across(other))
    after = (own,)
    attn_latent, done = attend_piece(
        cache_lengths, queries, latent_cache, LAT, 0, queries.shape[0] // PIECES, None, (block,)
    )
    for k in range(1, local_count):
        if k > 1:
            block = onward(block)
        own, other = run_experts(expert, (block,), (across(block),), gate, up, down, after)
        total = chip_sum(own, across(other))
        if k > 1:
            total += onward(running).astype(jnp.float32)
        running = total.astype(jnp.bfloat16)
        after = ()
        if done is not None:
            after, done = (done,), None
        if k < PIECES:
            attn_latent, done = attend_piece(
                cache_lengths,
                queries,
                latent_cache,
                LAT,
                k,
                queries.shape[0] // PIECES,
                attn_latent,
                (own,),
            )

    mine_sum = lax.optimization_barrier(
        jnp.where(first, mine_sum, jnp.concatenate([mine_sum[part:], mine_sum[:part]], axis=0))
    )
    same, cross = onward(running[:part]), onward(running[part:], hops_out)
    arrived = jnp.where(
        first, jnp.concatenate([same, cross], axis=0), jnp.concatenate([cross, same], axis=0)
    )
    moe_out = (mine_sum + arrived.astype(jnp.float32)).astype(jnp.bfloat16)

    return (moe_out, attn_latent)


def solution(mesh):
    in_specs = (
        P(("replica", "node", "local"), None),
        P(("replica", "node", "local"), None),
        P(("replica", "node", "local"), None),
        P(("node", "local"), None, None),
        P(("node", "local"), None, None),
        P(("node", "local"), None, None),
        P(("replica", "node", "local"), None, None),
        P(("replica", "node", "local"), None, None),
        P(("replica", "node", "local")),
    )
    out_specs = (P(("replica", "node", "local"), None), P(("replica", "node", "local"), None, None))
    return jax.shard_map(
        on_device, mesh=mesh, in_specs=in_specs, out_specs=out_specs, check_vma=False
    )
```

```python
import functools

import jax
import jax.numpy as jnp
from jax import lax
from jax.experimental import pallas as pl
from jax.experimental.pallas import tpu as pltpu
from jax.sharding import PartitionSpec as P

LAT = 512
SOFTMAX_SCALE = 192.0 ** (-0.5)
LANES = 128
PIECES = 8


def attend_kernel(len_ref, q_ref, c_ref, *rest, base, pair):
    done_ref = rest[-1]
    done_ref[...] = jnp.zeros_like(done_ref)
    out_ref = rest[-2]
    step, heads, wide = q_ref.shape
    slots = c_ref.shape[1]
    lat = out_ref.shape[2]
    row = lax.broadcasted_iota(jnp.int32, (pair * heads, pair * slots), 0) // heads
    col = lax.broadcasted_iota(jnp.int32, (pair * heads, pair * slots), 1)
    place = jnp.where(col // slots == row, col % slots, slots)
    which = lax.broadcasted_iota(jnp.int32, (pair * heads, 1), 0) // heads
    groups = range(0, step, pair)
    caches = [c_ref[at : at + pair].reshape(pair * slots, wide) for at in groups]
    scores = [
        lax.dot_general(
            q_ref[at : at + pair].reshape(pair * heads, wide),
            cache,
            (((1,), (1,)), ((), ())),
            preferred_element_type=jnp.float32,
        )
        for at, cache in zip(groups, caches, strict=True)
    ]
    probs = []
    for at, score in zip(groups, scores, strict=True):
        live = jnp.full((pair * heads, 1), len_ref[base + at], jnp.int32)
        for j in range(1, pair):
            live = jnp.where(which == j, len_ref[base + at + j], live)
        score = jnp.where(place < live, score * SOFTMAX_SCALE, -1e30)
        terms = jnp.exp(score - jnp.max(score, axis=1, keepdims=True))
        probs.append((terms * (1.0 / jnp.sum(terms, axis=1, keepdims=True))).astype(jnp.bfloat16))
    for at, prob, cache in zip(groups, probs, caches, strict=True):
        mixed = jnp.dot(prob, cache[:, :lat], preferred_element_type=jnp.float32)
        out_ref[at : at + pair] = mixed.astype(jnp.bfloat16).reshape(pair, heads, lat)


def attend_piece(lengths, queries, latent_cache, lat, piece, count, out, after):
    total, heads, wide = queries.shape
    slots = latent_cache.shape[1]

    def rows(middle, last):
        return pl.BlockSpec((count, middle, last), lambda i, n: (piece, 0, 0))

    extra = ([] if out is None else [out]) + list(after)
    return pl.pallas_call(
        functools.partial(attend_kernel, base=piece * count, pair=2),
        grid_spec=pltpu.PrefetchScalarGridSpec(
            num_scalar_prefetch=1,
            grid=(1,),
            in_specs=[rows(heads, wide), rows(slots, wide)]
            + [pl.BlockSpec(memory_space=pl.ANY)] * len(extra),
            out_specs=[rows(heads, lat), pl.BlockSpec((8, LANES), lambda i, n: (0, 0))],
        ),
        out_shape=[
            jax.ShapeDtypeStruct((total, heads, lat), jnp.bfloat16),
            jax.ShapeDtypeStruct((8, LANES), jnp.float32),
        ],
        input_output_aliases={} if out is None else {3: 0},
        compiler_params=pltpu.CompilerParams(vmem_limit_bytes=16 << 20),
        cost_estimate=pl.CostEstimate(
            flops=2 * count * heads * slots * (wide + lat),
            bytes_accessed=2 * count * (heads * (wide + lat) + slots * wide),
            transcendentals=count * heads * slots,
        ),
        name="attend",
    )(lengths, queries, latent_cache, *extra)


def expert_kernel(expert_ref, *refs, own_parts, parts):
    sources = refs[:parts]
    gate_ref, up_ref, down_ref = refs[parts : parts + 3]
    outs = refs[-2:]
    width = outs[0].shape[1]
    x = jnp.concatenate([source[:, :width] for source in sources], axis=0)
    gate = jnp.dot(x, gate_ref[...], preferred_element_type=jnp.float32)
    up = jnp.dot(x, up_ref[...], preferred_element_type=jnp.float32)
    hidden = (gate / (1.0 + jnp.exp(-gate)) * up).astype(jnp.bfloat16)
    down = jnp.dot(hidden, down_ref[...], preferred_element_type=jnp.float32)
    at = 0
    for i, source in enumerate(sources):
        rows = source.shape[0]
        lane = lax.broadcasted_iota(jnp.int32, (rows, LANES), 1)
        route = source[:, width:].astype(jnp.float32)
        weight = jnp.sum(jnp.where(lane == expert_ref[0], route, 0.0), axis=1, keepdims=True)
        out = outs[0] if i < own_parts else outs[1]
        to = at if i < own_parts else at - outs[0].shape[0]
        out[to : to + rows] = (weight * down[at : at + rows]).astype(jnp.bfloat16)
        at += rows


def run_experts(expert, own, other, gate, up, down, after=()):
    counts = [sum(part.shape[0] for part in parts) for parts in (own, other)]
    width, hidden = gate.shape
    inputs = (*own, *other, gate, up, down)
    return pl.pallas_call(
        functools.partial(
            expert_kernel, own_parts=len(own), parts=len(own) + len(other)
        ),
        grid_spec=pltpu.PrefetchScalarGridSpec(
            num_scalar_prefetch=1,
            grid=(1,),
            in_specs=[pl.BlockSpec(a.shape, lambda i, e: (0, 0)) for a in inputs]
            + [pl.BlockSpec(memory_space=pl.ANY)] * len(after),
            out_specs=[pl.BlockSpec((count, width), lambda i, e: (0, 0)) for count in counts],
        ),
        out_shape=[jax.ShapeDtypeStruct((count, width), jnp.bfloat16) for count in counts],
        compiler_params=pltpu.CompilerParams(vmem_limit_bytes=16 << 20),
        cost_estimate=pl.CostEstimate(
            flops=6 * sum(counts) * width * hidden,
            bytes_accessed=6 * width * hidden,
            transcendentals=sum(counts) * hidden,
        ),
        name="expert_half",
    )(expert, *inputs, *after)


def load_kernel(*refs, count):
    sources, targets, sems = refs[:count], refs[-count - 1 : -1], refs[-1]
    copies = [
        pltpu.make_async_copy(sources[i].at[0], targets[i], sems.at[i]) for i in range(count)
    ]
    for copy in copies:
        copy.start()
    for copy in copies:
        copy.wait()


def load_weights(weights, after):
    count = len(weights)
    anywhere = pl.BlockSpec(memory_space=pl.ANY)
    return pl.pallas_call(
        functools.partial(load_kernel, count=count),
        in_specs=[anywhere] * (count + len(after)),
        out_specs=[anywhere] * count,
        out_shape=[jax.ShapeDtypeStruct(w.shape[1:], w.dtype) for w in weights],
        scratch_shapes=[pltpu.SemaphoreType.DMA((count,))],
        compiler_params=pltpu.CompilerParams(vmem_limit_bytes=41 << 20),
        cost_estimate=pl.CostEstimate(
            flops=0, bytes_accessed=2 * sum(w.size for w in weights), transcendentals=0
        ),
        name="load_weights",
    )(*weights, *after)


def join_kernel(first_ref, second_ref, out_ref):
    rows = first_ref.shape[0]
    out_ref[:rows] = first_ref[...]
    out_ref[rows:] = second_ref[...]


def join(first, second):
    rows, width = first.shape
    return pl.pallas_call(
        join_kernel,
        grid=(1,),
        in_specs=[pl.BlockSpec((rows, width), lambda i: (0, 0))] * 2,
        out_specs=pl.BlockSpec((2 * rows, width), lambda i: (0, 0)),
        out_shape=jax.ShapeDtypeStruct((2 * rows, width), first.dtype),
        compiler_params=pltpu.CompilerParams(vmem_limit_bytes=16 << 20),
        name="join",
    )(first, second)


def ring_order(count):
    if count == 8:
        return [0, 2, 4, 6, 7, 5, 3, 1]
    return list(range(count))


def on_device(
    tokens, expert_ids, combine_weights, w_gate, w_up, w_down, queries, latent_cache, cache_lengths
):
    local_count = lax.axis_size("local")
    rows, width = tokens.shape
    part = rows // 2
    node = lax.axis_index("node")
    order = ring_order(local_count)
    hops, hops_out = [], []
    for i in range(local_count):
        here, there = order[i], order[(i + 1) % local_count]
        hops += [(here, there), (local_count + there, local_count + here)]
        hops_out += [(here, local_count + there), (local_count + there, here)]
    expert = ((node * local_count + lax.axis_index("local")) // 2).astype(jnp.int32).reshape(1)

    def onward(a, pairs=hops):
        return lax.ppermute(a, ("node", "local"), pairs)

    def across(a):
        return lax.ppermute(a, "node", [(0, 1), (1, 0)])

    def chip_sum(a, b):
        return a.astype(jnp.float32) + b.astype(jnp.float32)

    matches = expert_ids[:, :, None] == jnp.arange(LANES, dtype=jnp.int32)[None, None, :]
    route = jnp.sum(
        jnp.where(matches, combine_weights[:, :, None], jnp.zeros((), jnp.bfloat16)), axis=1
    )
    first = node == 0

    def halves(a):
        return jnp.where(first, a[:part], a[part:]), jnp.where(first, a[part:], a[:part])

    kept, given = [
        jnp.concatenate(pair, axis=1) for pair in zip(halves(tokens), halves(route), strict=True)
    ]
    swapped = across(given)
    gate, up, down = load_weights((w_gate, w_up, w_down), (kept,))
    block = join(onward(kept), onward(swapped))
    own, other = run_experts(
        expert, (kept, given), (across(kept), swapped), gate, up, down
    )
    block = lax.optimization_barrier((block, own))[0]
    mine_sum = chip_sum(own, across(other))
    after = (own,)
    attn_latent, done = attend_piece(
        cache_lengths, queries, latent_cache, LAT, 0, queries.shape[0] // PIECES, None, (block,)
    )
    for k in range(1, local_count):
        if k > 1:
            block = onward(block)
        own, other = run_experts(expert, (block,), (across(block),), gate, up, down, after)
        total = chip_sum(own, across(other))
        if k > 1:
            total += onward(running).astype(jnp.float32)
        running = total.astype(jnp.bfloat16)
        after = ()
        if done is not None:
            after, done = (done,), None
        if k < PIECES:
            attn_latent, done = attend_piece(
                cache_lengths,
                queries,
                latent_cache,
                LAT,
                k,
                queries.shape[0] // PIECES,
                attn_latent,
                (own,),
            )

    mine_sum = lax.optimization_barrier(
        jnp.where(first, mine_sum, jnp.concatenate([mine_sum[part:], mine_sum[:part]], axis=0))
    )
    same, cross = onward(running[:part]), onward(running[part:], hops_out)
    arrived = jnp.where(
        first, jnp.concatenate([same, cross], axis=0), jnp.concatenate([cross, same], axis=0)
    )
    moe_out = (mine_sum + arrived.astype(jnp.float32)).astype(jnp.bfloat16)

    return (moe_out, attn_latent)


def solution(mesh):
    in_specs = (
        P(("replica", "node", "local"), None),
        P(("replica", "node", "local"), None),
        P(("replica", "node", "local"), None),
        P(("node", "local"), None, None),
        P(("node", "local"), None, None),
        P(("node", "local"), None, None),
        P(("replica", "node", "local"), None, None),
        P(("replica", "node", "local"), None, None),
        P(("replica", "node", "local")),
    )
    out_specs = (P(("replica", "node", "local"), None), P(("replica", "node", "local"), None, None))
    return jax.shard_map(
        on_device, mesh=mesh, in_specs=in_specs, out_specs=out_specs, check_vma=False
    )
```
